256 devices in a mesh: aa: 8 (over x, z_lo), ba: 8 (over z_hi, core), col: 4 (over y).
Axes of the slice: x: 4, y: 4, z: 8 (z_hi: 4, z_lo: 2; z = z_hi * 2 + z_lo), core: 2. Of those that a mesh axis runs over, the one named last changes fastest.
Arguments:
- tokens: bfloat16 [5120, 5120], P(('aa', 'ba'), 'col'), may hold values from -6 to 6
- gate_weight: bfloat16 [6912, 5120], P(('aa', 'ba'), 'col'), may hold values from -0.078125 to 0.078125
- up_weight: bfloat16 [6912, 5120], P(('aa', 'ba'), 'col'), may hold values from -0.078125 to 0.078125
- down_weight: bfloat16 [6912, 5120], P(('aa', 'ba'), 'col'), may hold values from -0.078125 to 0.078125
- out_grad: bfloat16 [5120, 5120], P(('aa', 'ba'), 'col'), may hold values from -0.59765625 to 0.59765625
Outputs:
- mixed: bfloat16 [5120, 5120], P(('aa', 'ba'), 'col')
- input_grad: bfloat16 [5120, 5120], P(('aa', 'ba'), 'col')
- gate_weight_grad: bfloat16 [6912, 5120], P(('aa', 'ba'), 'col')
- up_weight_grad: bfloat16 [6912, 5120], P(('aa', 'ba'), 'col')
- down_weight_grad: bfloat16 [6912, 5120], P(('aa', 'ba'), 'col')
The draws below stay inside these ranges and needn't reach their ends.
All inputs are finite; a program needn't handle non-finite values.
Results may differ from the reference program's by a relative error of at most 0.028.
Values may be sent and summed in bfloat16 or wider, within the bound.
No kernel may reach another device: no remote copies, remote signals or barrier semaphores. Data moves between devices by JAX's collectives and lax.ppermute only.
A program may use at most 128 MiB of HBM per device.

```python
import jax
import jax.numpy as jnp
from jax import lax

D = 5120
FF = 6912
TOK_DEV = 80
TOKENS = 5120
N_AA = 8
N_BA = 8
N_COL = 4


def shard_levels(key, dims, split, smallest, top_value):
    level, own = 1.0, jax.random.fold_in(key, 6)
    for position, shards_of in split:
        draws = jnp.exp(jax.random.uniform(jax.random.fold_in(own, position), (shards_of,), jnp.float32, smallest / len(split), top_value / len(split)))
        level = level * jnp.repeat(draws, dims[position] // shards_of).reshape([-1 if axis == position else 1 for axis in range(len(dims))])
    return level


def noise(stream_key, shape, scale, reach, split=(), dtype=jnp.bfloat16):
    factor_of = shard_levels(stream_key, shape, split, -0.22, 0.18) if split else 1.0
    array = jax.random.normal(stream_key, shape, jnp.float32) * scale * factor_of
    return jnp.minimum(jnp.maximum(array, -reach), reach).astype(dtype)


def setup_inputs(seed: int = 0) -> dict:
    streams_of = jax.random.split(jax.random.key(seed), 6)
    tokens = noise(streams_of[0], (TOKENS, D), 1.0, 6.0, ((0, 64), (1, 4)))
    gate_weight = noise(streams_of[1], (FF, D), D ** -0.5, 0.078125, ((0, 64), (1, 4)))
    up_weight = noise(streams_of[2], (FF, D), D ** -0.5, 0.078125, ((0, 64), (1, 4)))
    down_weight = noise(streams_of[3], (FF, D), FF ** -0.5, 0.078125, ((0, 64), (1, 4)))
    out_grad = noise(streams_of[4], (TOKENS, D), 0.1, 0.59765625, ((0, 64), (1, 4)))
    return dict(tokens=tokens, gate_weight=gate_weight, up_weight=up_weight, down_weight=down_weight, out_grad=out_grad)


def rounded(value):
    return lax.optimization_barrier(value.astype(jnp.bfloat16)).astype(jnp.float32)


def block_sum(left, right, parts):
    width = left.shape[1] // parts
    total = jnp.zeros((left.shape[0], right.shape[1]), jnp.float32)
    for index in range(parts):
        product = jnp.dot(left[:, index * width:(index + 1) * width], right[index * width:(index + 1) * width], preferred_element_type=jnp.float32)
        total = total + rounded(product)
    return total


def group_sum(left, right):
    left_groups = left.reshape(N_AA, N_BA, TOK_DEV, left.shape[1])
    right_groups = right.reshape(N_AA, N_BA, TOK_DEV, right.shape[1])
    total = jnp.zeros((left.shape[1], right.shape[1]), jnp.float32)
    for group in range(N_BA):
        left_rows = left_groups[:, group].reshape(-1, left.shape[1])
        right_rows = right_groups[:, group].reshape(-1, right.shape[1])
        total = total + rounded(jnp.dot(left_rows.T, right_rows, preferred_element_type=jnp.float32))
    return total


def reference(tokens, gate_weight, up_weight, down_weight, out_grad):
    gate = block_sum(tokens, gate_weight.T, N_COL)
    up = block_sum(tokens, up_weight.T, N_COL)
    sig = jax.nn.sigmoid(gate)
    hidden = (gate * sig * up).astype(jnp.bfloat16)
    mixed = block_sum(hidden, down_weight, N_AA).astype(jnp.bfloat16)
    hidden_grad = block_sum(out_grad, down_weight.T, N_COL)
    gate_grad = (hidden_grad * up * sig * (1.0 + gate * (1.0 - sig))).astype(jnp.bfloat16)
    up_grad = (hidden_grad * gate * sig).astype(jnp.bfloat16)
    width = FF // N_AA
    input_total = jnp.zeros((tokens.shape[0], tokens.shape[1]), jnp.float32)
    for index in range(N_AA):
        lower = index * width
        upper = lower + width
        both = jnp.dot(gate_grad[:, lower:upper], gate_weight[lower:upper], preferred_element_type=jnp.float32)
        both = both + jnp.dot(up_grad[:, lower:upper], up_weight[lower:upper], preferred_element_type=jnp.float32)
        input_total = input_total + rounded(both)
    input_grad = input_total.astype(jnp.bfloat16)
    gate_weight_grad = group_sum(gate_grad, tokens).astype(jnp.bfloat16)
    up_weight_grad = group_sum(up_grad, tokens).astype(jnp.bfloat16)
    down_weight_grad = group_sum(hidden, out_grad).astype(jnp.bfloat16)
    return (mixed, input_grad, gate_weight_grad, up_weight_grad, down_weight_grad)
```

```python
import jax
import jax.numpy as jnp
from jax import lax
from jax.experimental import pallas as pl
from jax.experimental.pallas import tpu as pltpu
from jax.sharding import Mesh, PartitionSpec as P

BF = jnp.bfloat16
F32 = jnp.float32
Z = ("zl", "zh")
COLS = (((1,), (1,)), ((), ()))
PAD = 112
VMEM = 26 * 1024 * 1024


def bf(*shape):
    return jax.ShapeDtypeStruct(shape, BF)


def whole(*shape):
    return pl.BlockSpec(shape, lambda *_: (0,) * len(shape))


def call(kernel, args, ins, out, outs, name, grid=(1,), scratch=(), after=()):
    n, skip = len(args), len(after)
    return pl.pallas_call(
        lambda *refs: kernel(*refs[:n], *refs[n + skip :]),
        out_shape=out,
        grid=grid,
        in_specs=list(ins) + [pl.BlockSpec(memory_space=pl.ANY)] * skip,
        out_specs=outs,
        scratch_shapes=list(scratch),
        compiler_params=pltpu.CompilerParams(vmem_limit_bytes=VMEM),
        cost_estimate=pl.CostEstimate(flops=1024, bytes_accessed=1024, transcendentals=0),
        name=name,
    )(*args, *after)


STEPS = (0, 1, -1, 2)
BACK = (0, -1, 1, 2)
CUT = 48


def shift(value, axis, by):
    return lax.ppermute(value, axis, [(i, (i + by) % 4) for i in range(4)])


def swap(value):
    return lax.ppermute(value, "core", [(0, 1), (1, 0)])


def gather(block, axis):
    return [block] + [shift(block, axis, by) for by in STEPS[1:]]


def ring_gather(block, axis, cut):
    left, right = shift(block, axis, 1), shift(block, axis, -1)
    return [block, left, right, shift(left[:cut], axis, 1), shift(right[cut:], axis, -1)]


def scatter(pieces, axis, steps=STEPS):
    return [pieces[0]] + [shift(p, axis, by) for p, by in zip(pieces[1:], steps[1:])]


def slot_of(step):
    return lax.rem(lax.axis_index("y") + step + 4, 4)


def z_index(place):
    return (place % 2) * 4 + place // 2


def z_shift(value, by):
    return lax.ppermute(value, Z, [(z_index(i), z_index((i + by) % 8)) for i in range(8)])


def z_gather(block):
    fwd, bwd = [block], [block]
    for _ in range(3):
        fwd.append(z_shift(fwd[-1], 1))
        bwd.append(z_shift(bwd[-1], -1))
    half = block.shape[0] // 2
    return fwd + bwd[1:] + [z_shift(fwd[-1][:half], 1), z_shift(bwd[-1][half:], -1)]


def z_scatter(blocks, after):
    plus = lambda a, b: (a.astype(F32) + b.astype(F32)).astype(BF)
    far = later(blocks[4], after)
    up, down = z_shift(far[:CUT], 1), z_shift(far[CUT:], -1)
    up = jnp.concatenate([plus(blocks[3, :CUT], up), blocks[3, CUT:]], axis=0)
    down = jnp.concatenate([blocks[5, :CUT], plus(blocks[5, CUT:], down)], axis=0)
    for step in (2, 1):
        up, down = z_shift(up, 1), z_shift(down, -1)
        up, down = plus(blocks[step], up), plus(blocks[8 - step], down)
    up, down = z_shift(up, 1), z_shift(down, -1)
    return (blocks[0].astype(F32) + up.astype(F32) + down.astype(F32)).astype(BF)


def z_here():
    return 2 * lax.axis_index("zh") + lax.axis_index("zl")


def z_all(pieces):
    return lax.all_to_all(pieces, Z, split_axis=0, concat_axis=0)


def copy_kernel(x_ref, out_ref):
    out_ref[...] = x_ref[...]


def later(block, after):
    spec = whole(*block.shape)
    return call(copy_kernel, [block], [spec], bf(*block.shape), spec, "later", after=after)


def place_blocks(blocks, t_ref, g_ref):
    rows = t_ref.shape[1]
    for ref, step in zip(blocks[:7], (0, -1, -2, -3, 1, 2, 3)):
        place = z_index(lax.rem(z_here() + step + 8, 8))
        t_ref[place] = ref[:rows]
        g_ref[place] = ref[rows:]
    far = z_index(lax.rem(z_here() + 4, 8))
    t_ref[far] = blocks[7][...]
    g_ref[far] = blocks[8][...]


def project_rows(weights, place, rows, tok, outs, hold):
    for slot in range(4):
        for half, ref in enumerate(weights):
            left = ref[slot, place * rows : (place + 1) * rows]
            part = lax.dot_general(left, tok, COLS, preferred_element_type=F32)
            hold[slot, half * rows : (half + 1) * rows] = part.astype(BF)
    for out, step in zip(outs, STEPS):
        out[...] = hold[slot_of(step)]


def first_kernel(*refs):
    weights, blocks, (w_ref, t_ref, g_ref, *outs), hold = refs[:5], refs[5:14], refs[14:21], refs[21]
    for slot in range(3):
        w_ref[slot] = weights[slot][...]
    cut = weights[3].shape[0]
    w_ref[3, :cut] = weights[3][...]
    w_ref[3, cut:] = weights[4][...]
    place_blocks(blocks, t_ref, g_ref)
    project_rows([w_ref], 0, 2 * PAD, t_ref[...].reshape(-1, t_ref.shape[2]), outs, hold)


def project_first(weights, blocks):
    high, depth = weights[0].shape
    each, rows = blocks[0].shape[0] // 2, 2 * PAD
    n = 8 * each
    return call(
        first_kernel,
        [*weights, *blocks],
        [whole(*b.shape) for b in weights + blocks],
        (bf(4, high, depth), bf(8, each, depth), bf(8, each, depth)) + (bf(rows, n),) * 4,
        (whole(4, high, depth), whole(8, each, depth), whole(8, each, depth)) + (whole(rows, n),) * 4,
        "gate_up_own",
        scratch=[pltpu.VMEM((4, rows, n), BF)],
    )


def project_kernel(halves, place, rows, *refs):
    weights, t_ref, outs, hold = refs[:halves], refs[halves], refs[halves + 1 : halves + 5], refs[halves + 5]
    project_rows(weights, place, rows, t_ref[...].reshape(-1, t_ref.shape[2]), outs, hold)


def project(weights, place, rows, tok, name, after=()):
    n, high = 8 * tok.shape[1], rows * len(weights)
    return call(
        lambda *refs: project_kernel(len(weights), place, rows, *refs),
        [*weights, tok],
        [whole(*w.shape) for w in weights] + [whole(*tok.shape)],
        (bf(high, n),) * 4,
        (whole(high, n),) * 4,
        name,
        scratch=[pltpu.VMEM((4, high, n), BF)],
        after=after,
    )


def total(refs, rows):
    value = refs[0][rows, :].astype(F32)
    for ref in refs[1:]:
        value = value + ref[rows, :].astype(F32)
    return value


def hidden_kernel(*refs):
    parts, (share_ref, out_ref) = refs[:8], refs[8:]
    for half in range(2):
        start, own = 2 * PAD * half, parts[4 * half : 4 * half + 4]
        gate, up = total(own, slice(0, PAD)), total(own, slice(PAD, 2 * PAD))
        share_ref[start : start + PAD] = gate
        share_ref[start + PAD : start + 2 * PAD] = up
        sig = 1.0 / (1.0 + jnp.exp(-gate))
        out_ref[PAD * half : PAD * (half + 1)] = (gate * sig * up).astype(BF)


def make_hidden(parts):
    rows, n = parts[0].shape
    return call(
        hidden_kernel,
        parts,
        [whole(rows, n)] * 8,
        (jax.ShapeDtypeStruct((2 * rows, n), F32), bf(rows, n)),
        (whole(2 * rows, n), whole(rows, n)),
        "hidden",
    )


def grads_kernel(*refs):
    parts, share_ref, out_ref = refs[:4], refs[4], refs[5]
    for half in range(2):
        start = 2 * PAD * half
        hidden_grad = total(parts, slice(PAD * half, PAD * (half + 1)))
        gate, up = share_ref[start : start + PAD], share_ref[start + PAD : start + 2 * PAD]
        sig = 1.0 / (1.0 + jnp.exp(-gate))
        out_ref[start : start + PAD] = (hidden_grad * up * sig * (1.0 + gate * (1.0 - sig))).astype(BF)
        out_ref[start + PAD : start + 2 * PAD] = (hidden_grad * gate * sig).astype(BF)


def make_grads(parts, share):
    rows, n = parts[0].shape
    return call(
        grads_kernel,
        [*parts, share],
        [whole(rows, n)] * 4 + [whole(2 * rows, n)],
        bf(2 * rows, n),
        whole(2 * rows, n),
        "grads",
    )


def back_kernel(*refs):
    pieces, (own, other, out_ref, hold, turned) = refs[:4], refs[4:]

    @pl.when(pl.program_id(0) == 0)
    def _():
        for piece, step in zip(pieces, BACK):
            hold[slot_of(step)] = piece[...]
        turned[...] = hold[...].reshape(turned.shape[1], turned.shape[0]).T

    right = jnp.concatenate([ref[slot] for slot in range(4) for ref in (own, other)], axis=0)
    part = jnp.dot(turned[...], right, preferred_element_type=F32).astype(BF)
    if out_ref.ndim == 2:
        out_ref[...] = part
        return
    for index in range(8):
        place = 2 * (index % 4) + index // 4
        out_ref[lax.rem(place - z_here() + 8, 8)] = part[index * out_ref.shape[1] : (index + 1) * out_ref.shape[1]]


def back(pieces, own, other, place, name, by_place, after=()):
    high, n = pieces[0].shape
    rows, width, tile = high // 2, own.shape[2], 256
    spec = pl.BlockSpec((4, rows, tile), lambda i: (0, place, i))
    return call(
        back_kernel,
        [*pieces, own, other],
        [whole(high, n)] * 4 + [spec] * 2,
        bf(8, n // 8, width) if by_place else bf(n, width),
        pl.BlockSpec((8, n // 8, tile), lambda i: (0, 0, i)) if by_place else pl.BlockSpec((n, tile), lambda i: (0, i)),
        name,
        grid=(width // tile,),
        scratch=[pltpu.VMEM((4, high, n), BF), pltpu.VMEM((n, 4 * high), BF)],
        after=after,
    )


def outer_kernel(*refs):
    pieces, t_ref, out_ref, hold = refs[:4], refs[4], refs[5], refs[6]
    for piece, step in zip(pieces, BACK):
        hold[slot_of(step)] = piece[...]
    for slot in range(4):
        out_ref[slot] = jnp.dot(hold[slot], t_ref[...], preferred_element_type=F32).astype(BF)


def outer_add_kernel(*refs):
    pieces, t_ref, more_ref, outs, hold = refs[:4], refs[4], refs[5], refs[6:-1], refs[-1]
    for piece, step in zip(pieces, BACK):
        hold[slot_of(step)] = piece[...]
    for slot in range(4):
        part = jnp.dot(hold[slot], t_ref[...], preferred_element_type=F32)
        part = (part + more_ref[slot].astype(F32)).astype(BF)
        if len(outs) == 4:
            outs[slot][...] = part
        else:
            outs[0][lax.rem(lax.axis_index("x") + BACK[slot] + 4, 4)] = part


def outer(pieces, rows, place, tok, more, name, joined=False, after=()):
    n, width = tok.shape
    ins = [pl.BlockSpec((rows, n), lambda i: (place, 0))] * 4 + [whole(n, width)]
    scratch = [pltpu.VMEM((4, rows, n), BF)]
    if more is None:
        out, outs = bf(4, rows, width), whole(4, rows, width)
        return call(outer_kernel, [*pieces, tok], ins, out, outs, name, scratch=scratch, after=after)
    ins, out, outs = ins + [whole(4, rows, width)], (bf(rows, width),) * 4, (whole(rows, width),) * 4
    if joined:
        out, outs = bf(4, rows, width), whole(4, rows, width)
    return call(outer_add_kernel, [*pieces, tok, more], ins, out, outs, name, scratch=scratch, after=after)


def add_up(pieces):
    return sum(p.astype(F32) for p in pieces).astype(BF)


def body(tokens, gate_weight, up_weight, down_weight, out_grad):
    rows, width = tokens.shape
    pad = lambda w: jnp.pad(w, ((0, PAD - w.shape[0]), (0, 0)))
    weights = ring_gather(jnp.concatenate([pad(gate_weight), pad(up_weight), pad(down_weight)], axis=0), "x", 176)
    blocks = z_gather(jnp.concatenate([tokens, out_grad], axis=0))
    w, tok, grad, *gu_own = project_first(weights, blocks)
    x = swap(w)
    gu_own = scatter(gu_own, "y")
    gu_other = scatter(project([x], 0, 2 * PAD, tok, "gate_up_other"), "y")
    share, hidden = make_hidden(gu_own + gu_other)
    hg_parts = scatter(project([w, x], 2, PAD, grad, "hidden_grad", [hidden]), "y")
    hidden = gather(hidden, "y")
    grads = make_grads(hg_parts, share)
    shares = [grads]
    grads = gather(grads, "y")
    tok, grad = tok.reshape(8 * rows, width), grad.reshape(8 * rows, width)

    mixed_part = back(hidden, w, x, 2, "mixed", False, shares)
    mixed = add_up(list(z_all(mixed_part.reshape(8, rows, width))))
    down_more = swap(outer(hidden, PAD, 1, grad, None, "down_other", after=shares))
    down_part = outer(hidden, PAD, 0, grad, down_more, "down_own", after=[mixed_part])
    down_weight_grad = add_up(scatter(down_part, "x", BACK))[:108]

    gu_more = outer(grads, 2 * PAD, 1, tok, None, "gu_other", after=[down_weight_grad])
    input_part = back(grads, w, x, 0, "input", True, [gu_more, mixed])
    gu_part = outer(grads, 2 * PAD, 0, tok, swap(gu_more), "gu_own", True, [input_part])
    gu_grad = lax.all_to_all(gu_part, "x", split_axis=0, concat_axis=0).astype(F32).sum(0).astype(BF)
    input_grad = z_scatter(input_part, [gu_part])
    return (mixed, input_grad, gu_grad[:108], gu_grad[PAD : PAD + 108], down_weight_grad)


def solution(mesh):
    cube = Mesh(mesh.devices.reshape(4, 2, 4, 2, 4), ("x", "zl", "zh", "core", "y"))
    placed = P(("x", "zl", "zh", "core"), "y")
    return jax.shard_map(
        body, mesh=cube, in_specs=(placed,) * 5, out_specs=(placed,) * 5, check_vma=False
    )
```

```python
import jax
import jax.numpy as jnp
from jax import lax
from jax.experimental import pallas as pl
from jax.experimental.pallas import tpu as pltpu
from jax.sharding import Mesh, PartitionSpec as P

BF = jnp.bfloat16
F32 = jnp.float32
Z = ("zl", "zh")
COLS = (((1,), (1,)), ((), ()))
PAD = 112
VMEM = 26 * 1024 * 1024


def bf(*shape):
    return jax.ShapeDtypeStruct(shape, BF)


def whole(*shape):
    return pl.BlockSpec(shape, lambda *_: (0,) * len(shape))


def call(kernel, args, ins, out, outs, name, grid=(1,), scratch=(), after=()):
    n, skip = len(args), len(after)
    return pl.pallas_call(
        lambda *refs: kernel(*refs[:n], *refs[n + skip :]),
        out_shape=out,
        grid=grid,
        in_specs=list(ins) + [pl.BlockSpec(memory_space=pl.ANY)] * skip,
        out_specs=outs,
        scratch_shapes=list(scratch),
        compiler_params=pltpu.CompilerParams(vmem_limit_bytes=VMEM),
        cost_estimate=pl.CostEstimate(flops=1024, bytes_accessed=1024, transcendentals=0),
        name=name,
    )(*args, *after)


STEPS = (0, 1, -1, 2)
BACK = (0, -1, 1, 2)


def shift(value, axis, by):
    return lax.ppermute(value, axis, [(i, (i + by) % 4) for i in range(4)])


def plus(a, b):
    return (a.astype(F32) + b.astype(F32)).astype(BF)


def ring_scatter(pieces, axis):
    own, back, ahead, far = pieces
    cut = far.shape[0] // 2
    up, down = shift(far[:cut], axis, 1), shift(far[cut:], axis, -1)
    up = jnp.concatenate([plus(ahead[:cut], up), ahead[cut:]], axis=0)
    down = jnp.concatenate([back[:cut], plus(back[cut:], down)], axis=0)
    return [own, shift(up, axis, 1), shift(down, axis, -1)]


def swap(value):
    return lax.ppermute(value, "core", [(0, 1), (1, 0)])


def gather(block, axis):
    return [block] + [shift(block, axis, by) for by in STEPS[1:]]


def ring_gather(block, axis, cut):
    left, right = shift(block, axis, 1), shift(block, axis, -1)
    return [block, left, right, shift(left[:cut], axis, 1), shift(right[cut:], axis, -1)]


def scatter(pieces, axis, steps=STEPS):
    return [pieces[0]] + [shift(p, axis, by) for p, by in zip(pieces[1:], steps[1:])]


def slot_of(step):
    return lax.rem(lax.axis_index("y") + step + 4, 4)


def z_index(place):
    return (place % 2) * 4 + place // 2


def z_shift(value, by):
    return lax.ppermute(value, Z, [(z_index(i), z_index((i + by) % 8)) for i in range(8)])


def z_gather(block):
    fwd, bwd = [block], [block]
    for _ in range(3):
        fwd.append(z_shift(fwd[-1], 1))
        bwd.append(z_shift(bwd[-1], -1))
    half = block.shape[0] // 2
    return fwd + bwd[1:] + [z_shift(fwd[-1][:half], 1), z_shift(bwd[-1][half:], -1)]


def z_scatter(blocks, after):
    cut = blocks.shape[1] // 2
    far = later(blocks[4], after)
    up, down = z_shift(far[:cut], 1), z_shift(far[cut:], -1)
    up = jnp.concatenate([plus(blocks[3, :cut], up), blocks[3, cut:]], axis=0)
    down = jnp.concatenate([blocks[5, :cut], plus(blocks[5, cut:], down)], axis=0)
    for step in (2, 1):
        up, down = z_shift(up, 1), z_shift(down, -1)
        up, down = plus(blocks[step], up), plus(blocks[8 - step], down)
    return [blocks[0], z_shift(up, 1), z_shift(down, -1)]


def z_here():
    return 2 * lax.axis_index("zh") + lax.axis_index("zl")


def copy_kernel(x_ref, out_ref):
    out_ref[...] = x_ref[...]


def later(block, after):
    spec = whole(*block.shape)
    return call(copy_kernel, [block], [spec], bf(*block.shape), spec, "later", after=after)


def place_blocks(blocks, t_ref, g_ref):
    rows = t_ref.shape[1]
    for ref, step in zip(blocks[:7], (0, -1, -2, -3, 1, 2, 3)):
        place = z_index(lax.rem(z_here() + step + 8, 8))
        t_ref[place] = ref[:rows]
        g_ref[place] = ref[rows:]
    far = z_index(lax.rem(z_here() + 4, 8))
    t_ref[far] = blocks[7][...]
    g_ref[far] = blocks[8][...]


def project_rows(weights, place, rows, tok, outs, hold):
    for slot in range(4):
        for half, ref in enumerate(weights):
            left = ref[slot, place * rows : (place + 1) * rows]
            part = lax.dot_general(left, tok, COLS, preferred_element_type=F32)
            hold[slot, half * rows : (half + 1) * rows] = part.astype(BF)
    for out, step in zip(outs, STEPS):
        out[...] = hold[slot_of(step)]


def first_kernel(*refs):
    weights, blocks, (w_ref, t_ref, g_ref, *outs), hold = refs[:5], refs[5:14], refs[14:21], refs[21]
    for slot in range(3):
        w_ref[slot] = weights[slot][...]
    cut = weights[3].shape[0]
    w_ref[3, :cut] = weights[3][...]
    w_ref[3, cut:] = weights[4][...]
    place_blocks(blocks, t_ref, g_ref)
    project_rows([w_ref], 0, 2 * PAD, t_ref[...].reshape(-1, t_ref.shape[2]), outs, hold)


def project_first(weights, blocks):
    high, depth = weights[0].shape
    each, rows = blocks[0].shape[0] // 2, 2 * PAD
    n = 8 * each
    return call(
        first_kernel,
        [*weights, *blocks],
        [whole(*b.shape) for b in weights + blocks],
        (bf(4, high, depth), bf(8, each, depth), bf(8, each, depth)) + (bf(rows, n),) * 4,
        (whole(4, high, depth), whole(8, each, depth), whole(8, each, depth)) + (whole(rows, n),) * 4,
        "gate_up_own",
        scratch=[pltpu.VMEM((4, rows, n), BF)],
    )


def project_kernel(halves, place, rows, *refs):
    weights, t_ref, outs, hold = refs[:halves], refs[halves], refs[halves + 1 : halves + 5], refs[halves + 5]
    project_rows(weights, place, rows, t_ref[...].reshape(-1, t_ref.shape[2]), outs, hold)


def project(weights, place, rows, tok, name, after=()):
    n, high = 8 * tok.shape[1], rows * len(weights)
    return call(
        lambda *refs: project_kernel(len(weights), place, rows, *refs),
        [*weights, tok],
        [whole(*w.shape) for w in weights] + [whole(*tok.shape)],
        (bf(high, n),) * 4,
        (whole(high, n),) * 4,
        name,
        scratch=[pltpu.VMEM((4, high, n), BF)],
        after=after,
    )


def total(refs, rows):
    value = refs[0][rows, :].astype(F32)
    for ref in refs[1:]:
        value = value + ref[rows, :].astype(F32)
    return value


def hidden_kernel(*refs):
    parts, (share_ref, out_ref) = refs[:8], refs[8:]
    for half in range(2):
        start, own = 2 * PAD * half, parts[4 * half : 4 * half + 4]
        gate, up = total(own, slice(0, PAD)), total(own, slice(PAD, 2 * PAD))
        share_ref[start : start + PAD] = gate
        share_ref[start + PAD : start + 2 * PAD] = up
        sig = 1.0 / (1.0 + jnp.exp(-gate))
        out_ref[PAD * half : PAD * (half + 1)] = (gate * sig * up).astype(BF)


def make_hidden(parts, after):
    rows, n = parts[0].shape
    return call(
        hidden_kernel,
        parts,
        [whole(rows, n)] * 8,
        (jax.ShapeDtypeStruct((2 * rows, n), F32), bf(rows, n)),
        (whole(2 * rows, n), whole(rows, n)),
        "hidden",
        after=after,
    )


def grads_kernel(*refs):
    parts, share_ref, out_ref = refs[:4], refs[4], refs[5]
    for half in range(2):
        start = 2 * PAD * half
        hidden_grad = total(parts, slice(PAD * half, PAD * (half + 1)))
        gate, up = share_ref[start : start + PAD], share_ref[start + PAD : start + 2 * PAD]
        sig = 1.0 / (1.0 + jnp.exp(-gate))
        out_ref[start : start + PAD] = (hidden_grad * up * sig * (1.0 + gate * (1.0 - sig))).astype(BF)
        out_ref[start + PAD : start + 2 * PAD] = (hidden_grad * gate * sig).astype(BF)


def make_grads(parts, share):
    rows, n = parts[0].shape
    return call(
        grads_kernel,
        [*parts, share],
        [whole(rows, n)] * 4 + [whole(2 * rows, n)],
        bf(2 * rows, n),
        whole(2 * rows, n),
        "grads",
    )


def place_pieces(pieces, hold):
    for piece, step in zip(pieces[:3], BACK):
        hold[slot_of(step)] = piece[...]
    start = 0
    for piece in pieces[3:]:
        hold[slot_of(2), start : start + piece.shape[0]] = piece[...]
        start += piece.shape[0]


def back_kernel(count, *refs):
    pieces, own, other = refs[:count], refs[count], refs[count + 1]
    out_ref, hold, turned = refs[-3:]

    @pl.when(pl.program_id(0) == 0)
    def _():
        place_pieces(pieces, hold)
        turned[...] = hold[...].reshape(turned.shape[1], turned.shape[0]).T

    right = jnp.concatenate([ref[slot] for slot in range(4) for ref in (own, other)], axis=0)
    part = jnp.dot(turned[...], right, preferred_element_type=F32).astype(BF)
    each = part.shape[0] // 8
    for index in range(8):
        place = lax.rem(2 * (index % 4) + index // 4 - z_here() + 8, 8)
        part_here = part[index * each : (index + 1) * each]
        if len(refs) == count + 5:
            out_ref[place] = part_here
        else:
            out_ref[place, each:] = part_here
    if len(refs) > count + 5:
        out_ref[:, :each] = refs[count + 2][...]


def back(pieces, own, other, place, name, ahead=(), after=()):
    high, n = pieces[0].shape
    rows, width, tile = high // 2, own.shape[2], 256
    spec = pl.BlockSpec((4, rows, tile), lambda i: (0, place, i))
    turn = pl.BlockSpec((8, n // 8, tile), lambda i: (0, 0, i))
    each = (1 + len(ahead)) * n // 8
    return call(
        lambda *refs: back_kernel(len(pieces), *refs),
        [*pieces, own, other, *ahead],
        [whole(*p.shape) for p in pieces] + [spec] * 2 + [turn] * len(ahead),
        bf(8, each, width),
        pl.BlockSpec((8, each, tile), lambda i: (0, 0, i)),
        name,
        grid=(width // tile,),
        scratch=[pltpu.VMEM((4, high, n), BF), pltpu.VMEM((n, 4 * high), BF)],
        after=after,
    )


def outer_kernel(*refs):
    pieces, t_ref, out_ref, hold = refs[:4], refs[4], refs[5], refs[6]
    place_pieces(pieces, hold)
    for slot in range(4):
        out_ref[slot] = jnp.dot(hold[slot], t_ref[...], preferred_element_type=F32).astype(BF)


def outer_add_kernel(*refs):
    pieces, t_ref, more_ref, outs, hold = refs[:4], refs[4], refs[5], refs[6:-1], refs[-1]
    place_pieces(pieces, hold)
    for slot in range(4):
        part = jnp.dot(hold[slot], t_ref[...], preferred_element_type=F32)
        part = (part + more_ref[slot].astype(F32)).astype(BF)
        if len(outs) == 4:
            outs[slot][...] = part
        else:
            outs[0][lax.rem(lax.axis_index("x") + BACK[slot] + 4, 4)] = part


def outer(pieces, rows, place, tok, more, name, joined=False, after=()):
    n, width = tok.shape
    ins = [pl.BlockSpec((rows, n), lambda i: (place, 0))] * 3
    if len(pieces) == 4:
        ins.append(ins[0])
    else:
        pieces = [*pieces[:3], pieces[3 + place]]
        ins.append(whole(rows, n))
    ins.append(whole(n, width))
    scratch = [pltpu.VMEM((4, rows, n), BF)]
    if more is None:
        out, outs = bf(4, rows, width), whole(4, rows, width)
        return call(outer_kernel, [*pieces, tok], ins, out, outs, name, scratch=scratch, after=after)
    ins, out, outs = ins + [whole(4, rows, width)], (bf(rows, width),) * 4, (whole(rows, width),) * 4
    if joined:
        out, outs = bf(4, rows, width), whole(4, rows, width)
    return call(outer_add_kernel, [*pieces, tok, more], ins, out, outs, name, scratch=scratch, after=after)


def add_kernel(places, *refs):
    parts, outs = refs[: -len(places)], refs[-len(places) :]
    for place, out in zip(places, outs):
        out[...] = total(parts, slice(place, place + out.shape[0])).astype(BF)


def add_up(pieces, rows, places, name):
    width = pieces[0].shape[1]
    out = call(
        lambda *refs: add_kernel(places, *refs),
        pieces,
        [whole(*p.shape) for p in pieces],
        (bf(rows, width),) * len(places),
        (whole(rows, width),) * len(places),
        name,
    )
    return out


def add_slots(pieces, rows, places, name):
    _, high, width = pieces.shape
    return call(
        lambda *refs: add_kernel(places, *refs),
        [pieces] * 4,
        [pl.BlockSpec((None, high, width), lambda *_, slot=slot: (slot, 0, 0)) for slot in range(4)],
        (bf(rows, width),) * len(places),
        (whole(rows, width),) * len(places),
        name,
    )


def body(tokens, gate_weight, up_weight, down_weight, out_grad):
    rows, width = tokens.shape
    pad = lambda w: jnp.pad(w, ((0, PAD - w.shape[0]), (0, 0)))
    weights = ring_gather(jnp.concatenate([pad(gate_weight), pad(up_weight), pad(down_weight)], axis=0), "x", 176)
    blocks = z_gather(jnp.concatenate([tokens, out_grad], axis=0))
    w, tok, grad, *gu_own = project_first(weights, blocks)
    x = swap(w)
    gu_own = scatter(gu_own, "y")
    gu_other = scatter(project([x], 0, 2 * PAD, tok, "gate_up_other"), "y")
    hg_parts = project([w, x], 2, PAD, grad, "hidden_grad", gu_other[:1])
    share, hidden = make_hidden(gu_own + gu_other, hg_parts[:1])
    hg_parts = scatter(hg_parts, "y")
    hidden = gather(hidden, "y")
    grads_here = make_grads(hg_parts, share)
    grads = gather(grads_here, "y")
    tok, grad = tok.reshape(8 * rows, width), grad.reshape(8 * rows, width)

    mixed_part = back(hidden, w, x, 2, "mixed", after=[grads_here])
    down_more = swap(outer(hidden, PAD, 1, grad, None, "down_other", after=[grads_here]))
    down_part = outer(hidden, PAD, 0, grad, down_more, "down_own", after=[mixed_part])
    (down_weight_grad,) = add_up(scatter(down_part, "x", BACK), down_weight.shape[0], (0,), "down_sum")

    gu_more = outer(grads, 2 * PAD, 1, tok, None, "gu_other", after=[down_weight_grad])
    parts = back(grads, w, x, 0, "input", [mixed_part], [gu_more])
    gu_part = outer(grads, 2 * PAD, 0, tok, swap(gu_more), "gu_own", after=[parts])
    gate_weight_grad, up_weight_grad = add_up(ring_scatter(gu_part, "x"), gate_weight.shape[0], (0, PAD), "gu_sum")
    mixed, input_grad = add_up(z_scatter(parts, [gu_part[0]]), rows, (0, rows), "row_sum")
    return (mixed, input_grad, gate_weight_grad, up_weight_grad, down_weight_grad)


def solution(mesh):
    cube = Mesh(mesh.devices.reshape(4, 2, 4, 2, 4), ("x", "zl", "zh", "core", "y"))
    placed = P(("x", "zl", "zh", "core"), "y")
    return jax.shard_map(
        body, mesh=cube, in_specs=(placed,) * 5, out_specs=(placed,) * 5, check_vma=False
    )
```

```python
import jax
import jax.numpy as jnp
from jax import lax
from jax.experimental import pallas as pl
from jax.experimental.pallas import tpu as pltpu
from jax.sharding import Mesh, PartitionSpec as P

BF = jnp.bfloat16
F32 = jnp.float32
Z = ("zl", "zh")
COLS = (((1,), (1,)), ((), ()))
PAD = 112
VMEM = 26 * 1024 * 1024


def bf(*shape):
    return jax.ShapeDtypeStruct(shape, BF)


def whole(*shape):
    return pl.BlockSpec(shape, lambda *_: (0,) * len(shape))


def call(kernel, args, ins, out, outs, name, grid=(1,), scratch=(), after=()):
    n, skip = len(args), len(after)
    return pl.pallas_call(
        lambda *refs: kernel(*refs[:n], *refs[n + skip :]),
        out_shape=out,
        grid=grid,
        in_specs=list(ins) + [pl.BlockSpec(memory_space=pl.ANY)] * skip,
        out_specs=outs,
        scratch_shapes=list(scratch),
        compiler_params=pltpu.CompilerParams(vmem_limit_bytes=VMEM),
        cost_estimate=pl.CostEstimate(flops=1024, bytes_accessed=1024, transcendentals=0),
        name=name,
    )(*args, *after)


STEPS = (0, 1, -1, 2)
BACK = (0, -1, 1, 2)


def shift(value, axis, by):
    return lax.ppermute(value, axis, [(i, (i + by) % 4) for i in range(4)])


def plus(a, b):
    return (a.astype(F32) + b.astype(F32)).astype(BF)


def ring_scatter(pieces, axis):
    own, back, ahead, far = pieces
    cut = far.shape[0] // 2
    up, down = shift(far[:cut], axis, 1), shift(far[cut:], axis, -1)
    up = jnp.concatenate([plus(ahead[:cut], up), ahead[cut:]], axis=0)
    down = jnp.concatenate([back[:cut], plus(back[cut:], down)], axis=0)
    return [own, shift(up, axis, 1), shift(down, axis, -1)]


def swap(value):
    return lax.ppermute(value, "core", [(0, 1), (1, 0)])


def gather(block, axis):
    return [block] + [shift(block, axis, by) for by in STEPS[1:]]


def ring_gather(block, axis, cut):
    left, right = shift(block, axis, 1), shift(block, axis, -1)
    return [block, left, right, shift(left[:cut], axis, 1), shift(right[cut:], axis, -1)]


def scatter(pieces, axis, steps=STEPS):
    return [pieces[0]] + [shift(p, axis, by) for p, by in zip(pieces[1:], steps[1:])]


def slot_of(step):
    return lax.rem(lax.axis_index("y") + step + 4, 4)


def z_index(place):
    return (place % 2) * 4 + place // 2


def z_shift(value, by):
    return lax.ppermute(value, Z, [(z_index(i), z_index((i + by) % 8)) for i in range(8)])


def z_gather(block):
    fwd, bwd = [block], [block]
    for _ in range(3):
        fwd.append(z_shift(fwd[-1], 1))
        bwd.append(z_shift(bwd[-1], -1))
    half = block.shape[0] // 2
    return fwd + bwd[1:] + [z_shift(fwd[-1][:half], 1), z_shift(bwd[-1][half:], -1)]


def z_scatter(blocks, after):
    cut = blocks.shape[1] // 2
    far = later(blocks[4], after)
    up, down = z_shift(far[:cut], 1), z_shift(far[cut:], -1)
    up = jnp.concatenate([plus(blocks[3, :cut], up), blocks[3, cut:]], axis=0)
    down = jnp.concatenate([blocks[5, :cut], plus(blocks[5, cut:], down)], axis=0)
    for step in (2, 1):
        up, down = z_shift(up, 1), z_shift(down, -1)
        up, down = plus(blocks[step], up), plus(blocks[8 - step], down)
    return [blocks[0], z_shift(up, 1), z_shift(down, -1)]


def z_here():
    return 2 * lax.axis_index("zh") + lax.axis_index("zl")


def copy_kernel(x_ref, out_ref):
    out_ref[...] = x_ref[...]


def later(block, after):
    spec = whole(*block.shape)
    return call(copy_kernel, [block], [spec], bf(*block.shape), spec, "later", after=after)


def place_blocks(blocks, t_ref, g_ref):
    rows = t_ref.shape[1]
    for ref, step in zip(blocks[:7], (0, -1, -2, -3, 1, 2, 3)):
        place = z_index(lax.rem(z_here() + step + 8, 8))
        t_ref[place] = ref[:rows]
        g_ref[place] = ref[rows:]
    far = z_index(lax.rem(z_here() + 4, 8))
    t_ref[far] = blocks[7][...]
    g_ref[far] = blocks[8][...]


def project_rows(weights, place, rows, tok, outs, hold):
    for slot in range(4):
        for half, ref in enumerate(weights):
            left = ref[slot, place * rows : (place + 1) * rows]
            part = lax.dot_general(left, tok, COLS, preferred_element_type=F32)
            hold[slot, half * rows : (half + 1) * rows] = part.astype(BF)
    for out, step in zip(outs, STEPS):
        out[...] = hold[slot_of(step)]


def first_kernel(*refs):
    weights, blocks, (w_ref, t_ref, g_ref, *outs), hold = refs[:5], refs[5:14], refs[14:21], refs[21]
    for slot in range(3):
        w_ref[slot] = weights[slot][...]
    cut = weights[3].shape[0]
    w_ref[3, :cut] = weights[3][...]
    w_ref[3, cut:] = weights[4][...]
    place_blocks(blocks, t_ref, g_ref)
    project_rows([w_ref], 0, 2 * PAD, t_ref[...].reshape(-1, t_ref.shape[2]), outs, hold)


def project_first(weights, blocks):
    high, depth = weights[0].shape
    each, rows = blocks[0].shape[0] // 2, 2 * PAD
    n = 8 * each
    return call(
        first_kernel,
        [*weights, *blocks],
        [whole(*b.shape) for b in weights + blocks],
        (bf(4, high, depth), bf(8, each, depth), bf(8, each, depth)) + (bf(rows, n),) * 4,
        (whole(4, high, depth), whole(8, each, depth), whole(8, each, depth)) + (whole(rows, n),) * 4,
        "gate_up_own",
        scratch=[pltpu.VMEM((4, rows, n), BF)],
    )


def project_kernel(halves, place, rows, *refs):
    weights, t_ref, outs, hold = refs[:halves], refs[halves], refs[halves + 1 : halves + 5], refs[halves + 5]
    project_rows(weights, place, rows, t_ref[...].reshape(-1, t_ref.shape[2]), outs, hold)


def project(weights, place, rows, tok, name, after=()):
    n, high = 8 * tok.shape[1], rows * len(weights)
    return call(
        lambda *refs: project_kernel(len(weights), place, rows, *refs),
        [*weights, tok],
        [whole(*w.shape) for w in weights] + [whole(*tok.shape)],
        (bf(high, n),) * 4,
        (whole(high, n),) * 4,
        name,
        scratch=[pltpu.VMEM((4, high, n), BF)],
        after=after,
    )


def total(refs, rows):
    value = refs[0][rows, :].astype(F32)
    for ref in refs[1:]:
        value = value + ref[rows, :].astype(F32)
    return value


def hidden_kernel(*refs):
    parts, (share_ref, out_ref) = refs[:8], refs[8:]
    for half in range(2):
        start, own = 2 * PAD * half, parts[4 * half : 4 * half + 4]
        gate, up = total(own, slice(0, PAD)), total(own, slice(PAD, 2 * PAD))
        share_ref[start : start + PAD] = gate
        share_ref[start + PAD : start + 2 * PAD] = up
        sig = 1.0 / (1.0 + jnp.exp(-gate))
        out_ref[PAD * half : PAD * (half + 1)] = (gate * sig * up).astype(BF)


def make_hidden(parts, after):
    rows, n = parts[0].shape
    return call(
        hidden_kernel,
        parts,
        [whole(rows, n)] * 8,
        (jax.ShapeDtypeStruct((2 * rows, n), F32), bf(rows, n)),
        (whole(2 * rows, n), whole(rows, n)),
        "hidden",
        after=after,
    )


def grads_kernel(*refs):
    parts, share_ref, out_ref = refs[:4], refs[4], refs[5]
    for half in range(2):
        start = 2 * PAD * half
        hidden_grad = total(parts, slice(PAD * half, PAD * (half + 1)))
        gate, up = share_ref[start : start + PAD], share_ref[start + PAD : start + 2 * PAD]
        sig = 1.0 / (1.0 + jnp.exp(-gate))
        out_ref[start : start + PAD] = (hidden_grad * up * sig * (1.0 + gate * (1.0 - sig))).astype(BF)
        out_ref[start + PAD : start + 2 * PAD] = (hidden_grad * gate * sig).astype(BF)


def make_grads(parts, share):
    rows, n = parts[0].shape
    return call(
        grads_kernel,
        [*parts, share],
        [whole(rows, n)] * 4 + [whole(2 * rows, n)],
        bf(2 * rows, n),
        whole(2 * rows, n),
        "grads",
    )


def place_pieces(pieces, hold):
    for piece, step in zip(pieces[:3], BACK):
        hold[slot_of(step)] = piece[...]
    start = 0
    for piece in pieces[3:]:
        hold[slot_of(2), start : start + piece.shape[0]] = piece[...]
        start += piece.shape[0]


def back_kernel(count, *refs):
    pieces, own, other = refs[:count], refs[count], refs[count + 1]
    out_ref, hold, turned = refs[-3:]

    @pl.when(pl.program_id(0) == 0)
    def _():
        place_pieces(pieces, hold)
        turned[...] = hold[...].reshape(turned.shape[1], turned.shape[0]).T

    right = jnp.concatenate([ref[slot] for slot in range(4) for ref in (own, other)], axis=0)
    part = jnp.dot(turned[...], right, preferred_element_type=F32).astype(BF)
    each = part.shape[0] // 8
    for index in range(8):
        place = lax.rem(2 * (index % 4) + index // 4 - z_here() + 8, 8)
        part_here = part[index * each : (index + 1) * each]
        if len(refs) == count + 5:
            out_ref[place] = part_here
        else:
            out_ref[place, each:] = part_here
    if len(refs) > count + 5:
        out_ref[:, :each] = refs[count + 2][...]


def back(pieces, own, other, place, name, ahead=(), after=()):
    high, n = pieces[0].shape
    rows, width, tile = high // 2, own.shape[2], 256
    spec = pl.BlockSpec((4, rows, tile), lambda i: (0, place, i))
    turn = pl.BlockSpec((8, n // 8, tile), lambda i: (0, 0, i))
    each = (1 + len(ahead)) * n // 8
    return call(
        lambda *refs: back_kernel(len(pieces), *refs),
        [*pieces, own, other, *ahead],
        [whole(*p.shape) for p in pieces] + [spec] * 2 + [turn] * len(ahead),
        bf(8, each, width),
        pl.BlockSpec((8, each, tile), lambda i: (0, 0, i)),
        name,
        grid=(width // tile,),
        scratch=[pltpu.VMEM((4, high, n), BF), pltpu.VMEM((n, 4 * high), BF)],
        after=after,
    )


def outer_kernel(*refs):
    pieces, t_ref, out_ref, hold = refs[:4], refs[4], refs[5], refs[6]
    place_pieces(pieces, hold)
    for slot in range(4):
        out_ref[slot] = jnp.dot(hold[slot], t_ref[...], preferred_element_type=F32).astype(BF)


def outer_add_kernel(*refs):
    pieces, t_ref, more_ref, outs, hold = refs[:4], refs[4], refs[5], refs[6:-1], refs[-1]
    place_pieces(pieces, hold)
    for slot in range(4):
        part = jnp.dot(hold[slot], t_ref[...], preferred_element_type=F32)
        part = (part + more_ref[slot].astype(F32)).astype(BF)
        if len(outs) == 4:
            outs[slot][...] = part
        else:
            outs[0][lax.rem(lax.axis_index("x") + BACK[slot] + 4, 4)] = part


def outer(pieces, rows, place, tok, more, name, joined=False, after=()):
    n, width = tok.shape
    ins = [pl.BlockSpec((rows, n), lambda i: (place, 0))] * 3
    if len(pieces) == 4:
        ins.append(ins[0])
    else:
        pieces = [*pieces[:3], pieces[3 + place]]
        ins.append(whole(rows, n))
    ins.append(whole(n, width))
    scratch = [pltpu.VMEM((4, rows, n), BF)]
    if more is None:
        out, outs = bf(4, rows, width), whole(4, rows, width)
        return call(outer_kernel, [*pieces, tok], ins, out, outs, name, scratch=scratch, after=after)
    ins, out, outs = ins + [whole(4, rows, width)], (bf(rows, width),) * 4, (whole(rows, width),) * 4
    if joined:
        out, outs = bf(4, rows, width), whole(4, rows, width)
    return call(outer_add_kernel, [*pieces, tok, more], ins, out, outs, name, scratch=scratch, after=after)


def add_kernel(places, *refs):
    parts, outs = refs[: -len(places)], refs[-len(places) :]
    for place, out in zip(places, outs):
        out[...] = total(parts, slice(place, place + out.shape[0])).astype(BF)


def add_up(pieces, rows, places, name):
    width = pieces[0].shape[1]
    out = call(
        lambda *refs: add_kernel(places, *refs),
        pieces,
        [whole(*p.shape) for p in pieces],
        (bf(rows, width),) * len(places),
        (whole(rows, width),) * len(places),
        name,
    )
    return out


def add_slots(pieces, rows, places, name):
    _, high, width = pieces.shape
    return call(
        lambda *refs: add_kernel(places, *refs),
        [pieces] * 4,
        [pl.BlockSpec((None, high, width), lambda *_, slot=slot: (slot, 0, 0)) for slot in range(4)],
        (bf(rows, width),) * len(places),
        (whole(rows, width),) * len(places),
        name,
    )


def body(tokens, gate_weight, up_weight, down_weight, out_grad):
    rows, width = tokens.shape
    pad = lambda w: jnp.pad(w, ((0, PAD - w.shape[0]), (0, 0)))
    weights = ring_gather(jnp.concatenate([pad(gate_weight), pad(up_weight), pad(down_weight)], axis=0), "x", 176)
    blocks = z_gather(jnp.concatenate([tokens, out_grad], axis=0))
    w, tok, grad, *gu_own = project_first(weights, blocks)
    x = swap(w)
    gu_own = scatter(gu_own, "y")
    gu_other = scatter(project([x], 0, 2 * PAD, tok, "gate_up_other"), "y")
    hg_parts = project([w, x], 2, PAD, grad, "hidden_grad", gu_other[:1])
    share, hidden = make_hidden(gu_own + gu_other, hg_parts[:1])
    hg_parts = scatter(hg_parts, "y")
    hidden = gather(hidden, "y")
    grads_here = make_grads(hg_parts, share)
    grads = gather(grads_here, "y")
    tok, grad = tok.reshape(8 * rows, width), grad.reshape(8 * rows, width)

    mixed_part = back(hidden, w, x, 2, "mixed", after=[grads_here])
    down_more = swap(outer(hidden, PAD, 1, grad, None, "down_other", after=[grads_here]))
    gu_more = outer(grads, 2 * PAD, 1, tok, None, "gu_other", after=[mixed_part])
    parts = back(grads, w, x, 0, "input", [mixed_part], [gu_more])
    gu_part = outer(grads, 2 * PAD, 0, tok, swap(gu_more), "gu_own", after=[parts])
    gate_weight_grad, up_weight_grad = add_up(ring_scatter(gu_part, "x"), gate_weight.shape[0], (0, PAD), "gu_sum")
    down_part = outer(hidden, PAD, 0, grad, down_more, "down_own", after=[gu_part[0]])
    (down_weight_grad,) = add_up(scatter(down_part, "x", BACK), down_weight.shape[0], (0,), "down_sum")
    mixed, input_grad = add_up(z_scatter(parts, [gu_part[0]]), rows, (0, rows), "row_sum")
    return (mixed, input_grad, gate_weight_grad, up_weight_grad, down_weight_grad)


def solution(mesh):
    cube = Mesh(mesh.devices.reshape(4, 2, 4, 2, 4), ("x", "zl", "zh", "core", "y"))
    placed = P(("x", "zl", "zh", "core"), "y")
    return jax.shard_map(
        body, mesh=cube, in_specs=(placed,) * 5, out_specs=(placed,) * 5, check_vma=False
    )
```

```python
import jax
import jax.numpy as jnp
from jax import lax
from jax.experimental import pallas as pl
from jax.experimental.pallas import tpu as pltpu
from jax.sharding import Mesh, PartitionSpec as P

BF = jnp.bfloat16
F32 = jnp.float32
Z = ("zl", "zh")
COLS = (((1,), (1,)), ((), ()))
PAD = 112
VMEM = 26 * 1024 * 1024


def bf(*shape):
    return jax.ShapeDtypeStruct(shape, BF)


def whole(*shape):
    return pl.BlockSpec(shape, lambda *_: (0,) * len(shape))


def call(kernel, args, ins, out, outs, name, grid=(1,), scratch=(), after=()):
    n, skip = len(args), len(after)
    return pl.pallas_call(
        lambda *refs: kernel(*refs[:n], *refs[n + skip :]),
        out_shape=out,
        grid=grid,
        in_specs=list(ins) + [pl.BlockSpec(memory_space=pl.ANY)] * skip,
        out_specs=outs,
        scratch_shapes=list(scratch),
        compiler_params=pltpu.CompilerParams(vmem_limit_bytes=VMEM),
        cost_estimate=pl.CostEstimate(flops=1024, bytes_accessed=1024, transcendentals=0),
        name=name,
    )(*args, *after)


STEPS = (0, 1, -1, 2)
BACK = (0, -1, 1, 2)


def shift(value, axis, by):
    return lax.ppermute(value, axis, [(i, (i + by) % 4) for i in range(4)])


def plus(a, b):
    return (a.astype(F32) + b.astype(F32)).astype(BF)


def ring_scatter(pieces, axis):
    own, back, ahead, far = pieces
    cut = far.shape[0] // 2
    up, down = shift(far[:cut], axis, 1), shift(far[cut:], axis, -1)
    up = jnp.concatenate([plus(ahead[:cut], up), ahead[cut:]], axis=0)
    down = jnp.concatenate([back[:cut], plus(back[cut:], down)], axis=0)
    return [own, shift(up, axis, 1), shift(down, axis, -1)]


def swap(value):
    return lax.ppermute(value, "core", [(0, 1), (1, 0)])


def gather(block, axis):
    return [block] + [shift(block, axis, by) for by in STEPS[1:]]


def ring_gather(block, axis, cut):
    left, right = shift(block, axis, 1), shift(block, axis, -1)
    return [block, left, right, shift(left[:cut], axis, 1), shift(right[cut:], axis, -1)]


def scatter(pieces, axis, steps=STEPS):
    return [pieces[0]] + [shift(p, axis, by) for p, by in zip(pieces[1:], steps[1:])]


def slot_of(step):
    return lax.rem(lax.axis_index("y") + step + 4, 4)


def z_index(place):
    return (place % 2) * 4 + place // 2


def z_shift(value, by):
    return lax.ppermute(value, Z, [(z_index(i), z_index((i + by) % 8)) for i in range(8)])


def z_gather(block):
    fwd, bwd = [block], [block]
    for _ in range(3):
        fwd.append(z_shift(fwd[-1], 1))
        bwd.append(z_shift(bwd[-1], -1))
    half = block.shape[0] // 2
    return fwd + bwd[1:] + [z_shift(fwd[-1][:half], 1), z_shift(bwd[-1][half:], -1)]


def z_scatter(blocks, after):
    cut = blocks.shape[1] // 2
    far = later(blocks[4], after)
    up, down = z_shift(far[:cut], 1), z_shift(far[cut:], -1)
    up = jnp.concatenate([plus(blocks[3, :cut], up), blocks[3, cut:]], axis=0)
    down = jnp.concatenate([blocks[5, :cut], plus(blocks[5, cut:], down)], axis=0)
    for step in (2, 1):
        up, down = z_shift(up, 1), z_shift(down, -1)
        up, down = plus(blocks[step], up), plus(blocks[8 - step], down)
    return [blocks[0], z_shift(up, 1), z_shift(down, -1)]


def z_here():
    return 2 * lax.axis_index("zh") + lax.axis_index("zl")


def copy_kernel(x_ref, out_ref):
    out_ref[...] = x_ref[...]


def later(block, after):
    spec = whole(*block.shape)
    return call(copy_kernel, [block], [spec], bf(*block.shape), spec, "later", after=after)


def place_blocks(blocks, t_ref, g_ref):
    rows = t_ref.shape[1]
    for ref, step in zip(blocks[:7], (0, -1, -2, -3, 1, 2, 3)):
        place = z_index(lax.rem(z_here() + step + 8, 8))
        t_ref[place] = ref[:rows]
        g_ref[place] = ref[rows:]
    far = z_index(lax.rem(z_here() + 4, 8))
    t_ref[far] = blocks[7][...]
    g_ref[far] = blocks[8][...]


def project_rows(weights, place, rows, tok, outs, hold):
    for slot in range(4):
        for half, ref in enumerate(weights):
            left = ref[slot, place * rows : (place + 1) * rows]
            part = lax.dot_general(left, tok, COLS, preferred_element_type=F32)
            hold[slot, half * rows : (half + 1) * rows] = part.astype(BF)
    for out, step in zip(outs, STEPS):
        out[...] = hold[slot_of(step)]


def first_kernel(*refs):
    weights, blocks, (w_ref, t_ref, g_ref, *outs), hold = refs[:5], refs[5:14], refs[14:21], refs[21]
    for slot in range(3):
        w_ref[slot] = weights[slot][...]
    cut = weights[3].shape[0]
    w_ref[3, :cut] = weights[3][...]
    w_ref[3, cut:] = weights[4][...]
    place_blocks(blocks, t_ref, g_ref)
    project_rows([w_ref], 0, 2 * PAD, t_ref[...].reshape(-1, t_ref.shape[2]), outs, hold)


def project_first(weights, blocks):
    high, depth = weights[0].shape
    each, rows = blocks[0].shape[0] // 2, 2 * PAD
    n = 8 * each
    return call(
        first_kernel,
        [*weights, *blocks],
        [whole(*b.shape) for b in weights + blocks],
        (bf(4, high, depth), bf(8, each, depth), bf(8, each, depth)) + (bf(rows, n),) * 4,
        (whole(4, high, depth), whole(8, each, depth), whole(8, each, depth)) + (whole(rows, n),) * 4,
        "gate_up_own",
        scratch=[pltpu.VMEM((4, rows, n), BF)],
    )


def project_kernel(halves, place, rows, *refs):
    weights, t_ref, outs, hold = refs[:halves], refs[halves], refs[halves + 1 : halves + 5], refs[halves + 5]
    project_rows(weights, place, rows, t_ref[...].reshape(-1, t_ref.shape[2]), outs, hold)


def project(weights, place, rows, tok, name, after=()):
    n, high = 8 * tok.shape[1], rows * len(weights)
    return call(
        lambda *refs: project_kernel(len(weights), place, rows, *refs),
        [*weights, tok],
        [whole(*w.shape) for w in weights] + [whole(*tok.shape)],
        (bf(high, n),) * 4,
        (whole(high, n),) * 4,
        name,
        scratch=[pltpu.VMEM((4, high, n), BF)],
        after=after,
    )


def total(refs, rows):
    value = refs[0][rows, :].astype(F32)
    for ref in refs[1:]:
        value = value + ref[rows, :].astype(F32)
    return value


def hidden_kernel(*refs):
    parts, (share_ref, out_ref) = refs[:8], refs[8:]
    for half in range(2):
        start, own = 2 * PAD * half, parts[4 * half : 4 * half + 4]
        gate, up = total(own, slice(0, PAD)), total(own, slice(PAD, 2 * PAD))
        share_ref[start : start + PAD] = gate
        share_ref[start + PAD : start + 2 * PAD] = up
        sig = 1.0 / (1.0 + jnp.exp(-gate))
        out_ref[PAD * half : PAD * (half + 1)] = (gate * sig * up).astype(BF)


def make_hidden(parts, after):
    rows, n = parts[0].shape
    return call(
        hidden_kernel,
        parts,
        [whole(rows, n)] * 8,
        (jax.ShapeDtypeStruct((2 * rows, n), F32), bf(rows, n)),
        (whole(2 * rows, n), whole(rows, n)),
        "hidden",
        after=after,
    )


def grads_kernel(*refs):
    parts, share_ref, out_ref = refs[:4], refs[4], refs[5]
    for half in range(2):
        start = 2 * PAD * half
        hidden_grad = total(parts, slice(PAD * half, PAD * (half + 1)))
        gate, up = share_ref[start : start + PAD], share_ref[start + PAD : start + 2 * PAD]
        sig = 1.0 / (1.0 + jnp.exp(-gate))
        out_ref[start : start + PAD] = (hidden_grad * up * sig * (1.0 + gate * (1.0 - sig))).astype(BF)
        out_ref[start + PAD : start + 2 * PAD] = (hidden_grad * gate * sig).astype(BF)


def make_grads(parts, share):
    rows, n = parts[0].shape
    return call(
        grads_kernel,
        [*parts, share],
        [whole(rows, n)] * 4 + [whole(2 * rows, n)],
        bf(2 * rows, n),
        whole(2 * rows, n),
        "grads",
    )


def place_pieces(pieces, hold):
    for piece, step in zip(pieces[:3], BACK):
        hold[slot_of(step)] = piece[...]
    start = 0
    for piece in pieces[3:]:
        hold[slot_of(2), start : start + piece.shape[0]] = piece[...]
        start += piece.shape[0]


def back_kernel(count, *refs):
    pieces, own, other = refs[:count], refs[count], refs[count + 1]
    out_ref, hold, turned = refs[-3:]

    @pl.when(pl.program_id(0) == 0)
    def _():
        place_pieces(pieces, hold)
        turned[...] = hold[...].reshape(turned.shape[1], turned.shape[0]).T

    right = jnp.concatenate([ref[slot] for slot in range(4) for ref in (own, other)], axis=0)
    part = jnp.dot(turned[...], right, preferred_element_type=F32).astype(BF)
    each = part.shape[0] // 8
    for index in range(8):
        place = lax.rem(2 * (index % 4) + index // 4 - z_here() + 8, 8)
        part_here = part[index * each : (index + 1) * each]
        if len(refs) == count + 5:
            out_ref[place] = part_here
        else:
            out_ref[place, each:] = part_here
    if len(refs) > count + 5:
        out_ref[:, :each] = refs[count + 2][...]


def back(pieces, own, other, place, name, ahead=(), after=()):
    high, n = pieces[0].shape
    rows, width, tile = high // 2, own.shape[2], 256
    spec = pl.BlockSpec((4, rows, tile), lambda i: (0, place, i))
    turn = pl.BlockSpec((8, n // 8, tile), lambda i: (0, 0, i))
    each = (1 + len(ahead)) * n // 8
    return call(
        lambda *refs: back_kernel(len(pieces), *refs),
        [*pieces, own, other, *ahead],
        [whole(*p.shape) for p in pieces] + [spec] * 2 + [turn] * len(ahead),
        bf(8, each, width),
        pl.BlockSpec((8, each, tile), lambda i: (0, 0, i)),
        name,
        grid=(width // tile,),
        scratch=[pltpu.VMEM((4, high, n), BF), pltpu.VMEM((n, 4 * high), BF)],
        after=after,
    )


def outer_kernel(*refs):
    pieces, t_ref, out_ref, hold = refs[:4], refs[4], refs[5], refs[6]
    place_pieces(pieces, hold)
    for slot in range(4):
        out_ref[slot] = jnp.dot(hold[slot], t_ref[...], preferred_element_type=F32).astype(BF)


def outer_add_kernel(*refs):
    pieces, t_ref, more_ref, outs, hold = refs[:4], refs[4], refs[5], refs[6:-1], refs[-1]
    place_pieces(pieces, hold)
    for slot in range(4):
        part = jnp.dot(hold[slot], t_ref[...], preferred_element_type=F32)
        part = (part + more_ref[slot].astype(F32)).astype(BF)
        if len(outs) == 4:
            outs[slot][...] = part
        else:
            outs[0][lax.rem(lax.axis_index("x") + BACK[slot] + 4, 4)] = part


def outer(pieces, rows, place, tok, more, name, joined=False, after=()):
    n, width = tok.shape
    ins = [pl.BlockSpec((rows, n), lambda i: (place, 0))] * 3
    if len(pieces) == 4:
        ins.append(ins[0])
    else:
        pieces = [*pieces[:3], pieces[3 + place]]
        ins.append(whole(rows, n))
    ins.append(whole(n, width))
    scratch = [pltpu.VMEM((4, rows, n), BF)]
    if more is None:
        out, outs = bf(4, rows, width), whole(4, rows, width)
        return call(outer_kernel, [*pieces, tok], ins, out, outs, name, scratch=scratch, after=after)
    ins, out, outs = ins + [whole(4, rows, width)], (bf(rows, width),) * 4, (whole(rows, width),) * 4
    if joined:
        out, outs = bf(4, rows, width), whole(4, rows, width)
    return call(outer_add_kernel, [*pieces, tok, more], ins, out, outs, name, scratch=scratch, after=after)


def add_kernel(places, *refs):
    parts, outs = refs[: -len(places)], refs[-len(places) :]
    for place, out in zip(places, outs):
        out[...] = total(parts, slice(place, place + out.shape[0])).astype(BF)


def add_up(pieces, rows, places, name):
    width = pieces[0].shape[1]
    out = call(
        lambda *refs: add_kernel(places, *refs),
        pieces,
        [whole(*p.shape) for p in pieces],
        (bf(rows, width),) * len(places),
        (whole(rows, width),) * len(places),
        name,
    )
    return out


def add_slots(pieces, rows, places, name):
    _, high, width = pieces.shape
    return call(
        lambda *refs: add_kernel(places, *refs),
        [pieces] * 4,
        [pl.BlockSpec((None, high, width), lambda *_, slot=slot: (slot, 0, 0)) for slot in range(4)],
        (bf(rows, width),) * len(places),
        (whole(rows, width),) * len(places),
        name,
    )


def body(tokens, gate_weight, up_weight, down_weight, out_grad):
    rows, width = tokens.shape
    pad = lambda w: jnp.pad(w, ((0, PAD - w.shape[0]), (0, 0)))
    weights = ring_gather(jnp.concatenate([pad(gate_weight), pad(up_weight), pad(down_weight)], axis=0), "x", 176)
    blocks = z_gather(jnp.concatenate([tokens, out_grad], axis=0))
    w, tok, grad, *gu_own = project_first(weights, blocks)
    x = swap(w)
    gu_own = scatter(gu_own, "y")
    gu_other = scatter(project([x], 0, 2 * PAD, tok, "gate_up_other"), "y")
    hg_parts = project([w, x], 2, PAD, grad, "hidden_grad", gu_other[:1])
    share, hidden = make_hidden(gu_own + gu_other, hg_parts[:1])
    hg_parts = scatter(hg_parts, "y")
    hidden = gather(hidden, "y")
    grads_here = make_grads(hg_parts, share)
    grads = gather(grads_here, "y")
    tok, grad = tok.reshape(8 * rows, width), grad.reshape(8 * rows, width)

    mixed_part = back(hidden, w, x, 2, "mixed", after=[grads_here])
    down_more = swap(outer(hidden, PAD, 1, grad, None, "down_other", after=[grads_here]))
    down_part = outer(hidden, PAD, 0, grad, down_more, "down_own", after=[mixed_part])
    (down_weight_grad,) = add_up(scatter(down_part, "x", BACK), down_weight.shape[0], (0,), "down_sum")
    gu_more = outer(grads, 2 * PAD, 1, tok, None, "gu_other", after=[down_part[0]])
    parts = back(grads, w, x, 0, "input", [mixed_part], [gu_more])
    gu_part = outer(grads, 2 * PAD, 0, tok, swap(gu_more), "gu_own", after=[parts])
    gate_weight_grad, up_weight_grad = add_up(ring_scatter(gu_part, "x"), gate_weight.shape[0], (0, PAD), "gu_sum")
    mixed, input_grad = add_up(z_scatter(parts, [gu_part[0]]), rows, (0, rows), "row_sum")
    return (mixed, input_grad, gate_weight_grad, up_weight_grad, down_weight_grad)


def solution(mesh):
    cube = Mesh(mesh.devices.reshape(4, 2, 4, 2, 4), ("x", "zl", "zh", "core", "y"))
    placed = P(("x", "zl", "zh", "core"), "y")
    return jax.shard_map(
        body, mesh=cube, in_specs=(placed,) * 5, out_specs=(placed,) * 5, check_vma=False
    )
```
